32 devices in a mesh: groups: 2 (over y), inp: 8 (over z, x), out: 2 (over core).
Axes of the slice: x: 2, y: 2, z: 4, core: 2. Of those that a mesh axis runs over, the one named last changes fastest.
Arguments:
- tokens: bfloat16 [16, 16384], P('groups', 'inp'), parts along dimension 0, may hold values from -6 to 6
- norm_gain: bfloat16 [16384], P('inp'), may hold values from 0.5 to 1.5
- positions: int32 [16], P('groups'), parts along dimension 0, may hold values from 0 to 7, as said below
- w_query: bfloat16 [16384, 8192], P('inp', 'out'), may hold values from -0.046875 to 0.046875
- key_weight: bfloat16 [16384, 512], P('inp', 'out'), may hold values from -0.046875 to 0.046875
- value_weight: bfloat16 [16384, 512], P('inp', 'out'), may hold values from -0.046875 to 0.046875
- w_output: bfloat16 [8192, 16384], P('out', 'inp'), may hold values from -0.25 to 0.25
Outputs:
- block_out: bfloat16 [16, 16384], P(('groups', 'out'), 'inp'), parts along dimension 0
The draws below stay inside these ranges and needn't reach their ends.
There are 2 independent parts, one for each index of `groups`. The reference program is written for one: setup_inputs(seed, part) draws one part's arguments, and reference() takes and returns one part's arrays. A program takes and returns all parts, laid end to end along the dimension named above; an argument that names none is the same for every part. Nothing has to cross between parts.
Inputs may be any that keep to these rules, and one draw needn't show every extreme that they name: `positions`: each entry is either 0 (a new document) or one more than the entry before it; the stretch's first document covers more than 4 tokens and ends at position 7.
All inputs are finite; a program needn't handle non-finite values.
Results may differ from the reference program's by a relative error of at most 0.0071.
Values may be sent and summed in bfloat16 or wider, within the bound.
A program may use at most 128 MiB of HBM per device.

```python
import jax
import jax.numpy as jnp
from jax import lax

MODEL_WIDTH = 16384
QUERY_HEADS = 64
LOCAL_KEY_HEADS = 4
HEAD_SIZE = 128
TOKENS = 8


def draw_positions(key, part):
    key = jax.random.fold_in(key, 7)
    first_key = jax.random.fold_in(key, 1)
    coin_key = jax.random.fold_in(key, 2)
    index_all = jnp.arange(TOKENS, dtype=jnp.int32)
    first_len = jax.random.randint(first_key, (), TOKENS // 2 + 1, TOKENS + 1).astype(jnp.int32)
    coin = jax.random.randint(coin_key, (TOKENS,), 0, 8)
    begins = (index_all == first_len) | (coin == 0) & (index_all > first_len)
    latest = lax.cummax(jnp.where(begins, index_all, 0), axis=0)
    later = index_all - latest
    opening = index_all + TOKENS - first_len
    return jnp.where(index_all < first_len, opening, later).astype(jnp.int32)


def levels(own_key, dims, pieces, low, largest):
    loudness = 1.0
    for axis_at, parts in pieces:
        steps = jax.random.uniform(jax.random.fold_in(jax.random.fold_in(own_key, 6), axis_at), (parts,), jnp.float32, low / len(pieces), largest / len(pieces))
        loudness = loudness * jnp.repeat(jnp.exp(steps), dims[axis_at] // parts).reshape((-1,) + (1,) * (len(dims) - 1 - axis_at))
    return loudness


def gaussian(own_key, extent, scale, bound, pieces=(), kind=jnp.bfloat16):
    result = scale * jax.random.normal(own_key, extent, jnp.float32)
    if pieces:
        result = result * levels(own_key, extent, pieces, -0.22, 0.18)
    return jnp.clip(result, -bound, bound).astype(kind)


def setup_inputs(seed: int = 0, part: int = 0) -> dict:
    arg_keys = jax.random.split(jax.random.key(seed), 8)
    part_splits = jax.random.split(jax.random.fold_in(arg_keys[7], part), 8)
    return {
        "tokens": gaussian(part_splits[0], (TOKENS, MODEL_WIDTH), 1.0, 6.0, ((1, 8),)),
        "norm_gain": jnp.clip(1.0 + 0.1 * jax.random.normal(arg_keys[1], (MODEL_WIDTH,), jnp.float32), 0.5, 1.5).astype(jnp.bfloat16),
        "positions": draw_positions(jax.random.fold_in(jax.random.fold_in(arg_keys[7], part), 71), part),
        "w_query": gaussian(arg_keys[3], (MODEL_WIDTH, QUERY_HEADS * HEAD_SIZE), MODEL_WIDTH ** -0.5, 0.046875, ((0, 8), (1, 2))),
        "key_weight": gaussian(arg_keys[4], (MODEL_WIDTH, LOCAL_KEY_HEADS * HEAD_SIZE), MODEL_WIDTH ** -0.5, 0.046875, ((0, 8), (1, 2))),
        "value_weight": gaussian(arg_keys[5], (MODEL_WIDTH, LOCAL_KEY_HEADS * HEAD_SIZE), MODEL_WIDTH ** -0.5, 0.046875, ((0, 8), (1, 2))),
        "w_output": gaussian(arg_keys[6], (QUERY_HEADS * HEAD_SIZE, MODEL_WIDTH), (4 * HEAD_SIZE) ** -0.5, 0.25, ((0, 2), (1, 8))),
    }


THETA = 500000.0

def apply_rotary(values_in, pos):
    half = values_in.shape[-1] // 2
    index_f = jnp.arange(half, dtype=jnp.float32)
    freq = jnp.exp(-jnp.log(jnp.float32(THETA)) * 2.0 * index_f / (2.0 * half))
    angle = pos.astype(jnp.float32)[:, None] * freq[None, :]
    cosine = jnp.cos(angle)[:, None, :]
    sine = jnp.sin(angle)[:, None, :]
    first = values_in[..., :half]
    second = values_in[..., half:]
    return jnp.concatenate([first * cosine - second * sine, second * cosine + first * sine], axis=-1)

def reference(tokens, norm_gain, positions, w_query, key_weight, value_weight, w_output):
    partial_total = tokens.shape[0]
    query_group = QUERY_HEADS // LOCAL_KEY_HEADS
    token_f = tokens.astype(jnp.float32)
    scale = lax.rsqrt(lax.optimization_barrier(jnp.mean(token_f * token_f, axis=1)) + 1e-05)
    normed = (token_f * scale[:, None] * norm_gain.astype(jnp.float32)[None, :]).astype(jnp.bfloat16)
    query = jnp.dot(normed, w_query, preferred_element_type=jnp.float32).astype(jnp.bfloat16)
    key_matrix = jnp.dot(normed, key_weight, preferred_element_type=jnp.float32).astype(jnp.bfloat16)
    value_matrix = jnp.dot(normed, value_weight, preferred_element_type=jnp.float32).astype(jnp.bfloat16)
    rotated_query = apply_rotary(query.astype(jnp.float32).reshape(partial_total, QUERY_HEADS, HEAD_SIZE), positions).astype(jnp.bfloat16)
    rotated_keys = apply_rotary(key_matrix.astype(jnp.float32).reshape(partial_total, LOCAL_KEY_HEADS, HEAD_SIZE), positions).astype(jnp.bfloat16)
    query_per_head = rotated_query.reshape(partial_total, LOCAL_KEY_HEADS, query_group, HEAD_SIZE).transpose(1, 2, 0, 3)
    key_heads = rotated_keys.transpose(1, 0, 2)
    value_per_head = value_matrix.reshape(partial_total, LOCAL_KEY_HEADS, HEAD_SIZE).transpose(1, 0, 2)
    rows = jnp.arange(partial_total, dtype=jnp.int32)[:, None]
    cols = jnp.arange(partial_total, dtype=jnp.int32)[None, :]
    allowed = (cols <= rows) & (rows - cols <= positions[:, None])

    def one_head(packed):
        q_block, k_block, v_block = packed
        scores = jnp.einsum('gtd,sd->gts', q_block.astype(jnp.float32), k_block.astype(jnp.float32)) / jnp.sqrt(jnp.float32(HEAD_SIZE))
        scores = jnp.where(allowed[None], scores, jnp.float32(-1e+30))
        expo = jnp.exp(scores)
        probs = (expo / lax.optimization_barrier(jnp.sum(expo, axis=-1, keepdims=True))).astype(jnp.bfloat16)
        return jnp.einsum('gts,sd->gtd', probs.astype(jnp.float32), v_block.astype(jnp.float32)).astype(jnp.bfloat16)
    context = lax.map(one_head, (query_per_head, key_heads, value_per_head))
    context = context.transpose(2, 0, 1, 3).reshape(partial_total, QUERY_HEADS * HEAD_SIZE)
    product = jnp.dot(context, w_output, preferred_element_type=jnp.float32)
    return (product + token_f).astype(jnp.bfloat16)
```

```python
import functools
import math

import jax
import jax.numpy as jnp
from jax import lax
from jax.experimental import pallas as pl
from jax.experimental.pallas import tpu as pltpu
from jax.sharding import PartitionSpec as P

MODEL_WIDTH = 16384
HEAD_SIZE = 128


THETA = 500000.0


def apply_rotary(flat, pos):
    rows = flat.shape[0]
    heads = flat.shape[1] // HEAD_SIZE
    half = HEAD_SIZE // 2
    shaped = flat.astype(jnp.float32).reshape(rows, heads, HEAD_SIZE)
    index_f = jnp.arange(half, dtype=jnp.float32)
    freq = jnp.exp(-jnp.log(jnp.float32(THETA)) * 2.0 * index_f / (2.0 * half))
    angle = pos.astype(jnp.float32)[:, None] * freq[None, :]
    cosine = jnp.cos(angle)[:, None, :]
    sine = jnp.sin(angle)[:, None, :]
    first = shaped[..., :half]
    second = shaped[..., half:]
    turned = jnp.concatenate(
        [first * cosine - second * sine, second * cosine + first * sine], axis=-1
    )
    return turned.reshape(rows, heads * HEAD_SIZE).astype(jnp.bfloat16)


def attend(rotated_query, row_pos, row_index, rotated_keys, value_matrix):
    rows = rotated_query.shape[0]
    partial_total = rotated_keys.shape[0]
    kv_heads = rotated_keys.shape[1] // HEAD_SIZE
    query_group = rotated_query.shape[1] // HEAD_SIZE // kv_heads
    q_shaped = rotated_query.reshape(rows, kv_heads, query_group, HEAD_SIZE)
    k_shaped = rotated_keys.reshape(partial_total, kv_heads, HEAD_SIZE)
    v_shaped = value_matrix.reshape(partial_total, kv_heads, HEAD_SIZE)
    scores = jnp.einsum("rkgd,skd->rkgs", q_shaped, k_shaped, preferred_element_type=jnp.float32)
    scores = scores / jnp.sqrt(jnp.float32(HEAD_SIZE))
    cols = jnp.arange(partial_total, dtype=jnp.int32)[None, :]
    allowed = (cols <= row_index[:, None]) & (row_index[:, None] - cols <= row_pos[:, None])
    scores = jnp.where(allowed[:, None, None, :], scores, jnp.float32(-1e30))
    expo = jnp.exp(scores)
    probs = (expo / jnp.sum(expo, axis=-1, keepdims=True)).astype(jnp.bfloat16)
    context = jnp.einsum("rkgs,skd->rkgd", probs, v_shaped, preferred_element_type=jnp.float32)
    return context.astype(jnp.bfloat16).reshape(rows, kv_heads * query_group * HEAD_SIZE)


def shards(tokens, norm_gain, positions, w_query, key_weight, value_weight, w_output):
    partial_total = tokens.shape[0]
    token_f = tokens.astype(jnp.float32)
    squares = lax.psum(jnp.sum(token_f * token_f, axis=1), "inp")
    scale = lax.rsqrt(squares / MODEL_WIDTH + 1e-05)
    normed = (token_f * scale[:, None] * norm_gain.astype(jnp.float32)[None, :]).astype(
        jnp.bfloat16
    )
    query_width = w_query.shape[1]
    q_part = jnp.dot(normed, w_query, preferred_element_type=jnp.float32)
    k_part = jnp.dot(normed, key_weight, preferred_element_type=jnp.float32)
    v_part = jnp.dot(normed, value_weight, preferred_element_type=jnp.float32)
    q_sum, k_sum, v_sum = lax.psum((q_part, k_part, v_part), "inp")
    rotated_query = apply_rotary(q_sum.astype(jnp.bfloat16), positions)
    rotated_keys = apply_rotary(k_sum.astype(jnp.bfloat16), positions)
    value_matrix = v_sum.astype(jnp.bfloat16)
    block_rows = min(partial_total, 128)
    blocks = partial_total // block_rows
    index_all = jnp.arange(partial_total, dtype=jnp.int32)

    def one_block(packed):
        q_block, pos_block, index_block = packed
        return attend(q_block, pos_block, index_block, rotated_keys, value_matrix)

    context = lax.map(
        one_block,
        (
            rotated_query.reshape(blocks, block_rows, query_width),
            positions.reshape(blocks, block_rows),
            index_all.reshape(blocks, block_rows),
        ),
    )
    context = context.reshape(partial_total, query_width)
    partial_out = jnp.dot(context, w_output, preferred_element_type=jnp.float32)
    reduced = lax.psum_scatter(partial_out, "out", scatter_dimension=0, tiled=True)
    half_rows = reduced.shape[0]
    residual = lax.dynamic_slice_in_dim(token_f, lax.axis_index("out") * half_rows, half_rows, 0)
    return (reduced + residual).astype(jnp.bfloat16)


MESH = pl.DeviceIdType.MESH


def neighbour_at(me, step, count):
    offset = ((step + 1) // 2) * (2 * (step % 2) - 1)
    return (me + offset + count) % count


def fused_kernel(
    count,
    pos_ref,
    tok_ref,
    gain_ref,
    wq_hbm,
    wk_hbm,
    wv_hbm,
    wo_hbm,
    out_ref,
    wq,
    wkv,
    wo,
    x_buf,
    kv_buf,
    squares,
    part_out,
    part_in,
    own_part,
    ctx_all,
    swap_out,
    swap_in,
    wq_sem,
    wkv_sem,
    wo_sem,
    sq_send,
    sq_recv,
    part_send,
    part_recv,
    ctx_send,
    ctx_recv,
    swap_sem,
):
    me = lax.axis_index("inp")
    core = lax.axis_index("out")
    rows = tok_ref.shape[0]
    width = wq.shape[2]
    heads = width // HEAD_SIZE
    kv_width = wk_hbm.shape[1]
    kv_heads = kv_width // HEAD_SIZE
    per_kv = count // kv_heads

    def wq_copy(chunk):
        cols = pl.ds(pl.multiple_of(chunk * width, width), width)
        return pltpu.make_async_copy(wq_hbm.at[:, cols], wq.at[chunk], wq_sem.at[chunk])

    def wo_copy(chunk):
        at = pl.ds(pl.multiple_of(chunk * width, width), width)
        return pltpu.make_async_copy(wo_hbm.at[at, :], wo.at[chunk], wo_sem.at[chunk])

    def wk_copy():
        return pltpu.make_async_copy(wk_hbm, wkv.at[:, 0:kv_width], wkv_sem.at[0])

    def wv_copy():
        return pltpu.make_async_copy(wv_hbm, wkv.at[:, kv_width : 2 * kv_width], wkv_sem.at[1])

    def sq_copy(other):
        return pltpu.make_async_remote_copy(
            src_ref=squares.at[me],
            dst_ref=squares.at[me],
            send_sem=sq_send.at[other],
            recv_sem=sq_recv.at[me],
            device_id={"inp": other},
            device_id_type=MESH,
        )

    def part_copy(other):
        return pltpu.make_async_remote_copy(
            src_ref=part_out.at[other],
            dst_ref=part_in.at[me],
            send_sem=part_send.at[other],
            recv_sem=part_recv.at[me],
            device_id={"inp": other},
            device_id_type=MESH,
        )

    def ctx_copy(other):
        return pltpu.make_async_remote_copy(
            src_ref=ctx_all.at[me],
            dst_ref=ctx_all.at[me],
            send_sem=ctx_send.at[other],
            recv_sem=ctx_recv.at[me],
            device_id={"inp": other},
            device_id_type=MESH,
        )

    def arrival(buffer, send, recv, other):
        return pltpu.make_async_remote_copy(
            src_ref=buffer.at[other],
            dst_ref=buffer.at[other],
            send_sem=send.at[other],
            recv_sem=recv.at[other],
            device_id={"inp": other},
            device_id_type=MESH,
        )

    wk_copy().start()
    wv_copy().start()
    for step in range(count - 1, -1, -1):
        wq_copy(neighbour_at(me, step, count)).start()

    barrier = pltpu.get_barrier_semaphore()
    for step in range(1, count):
        other = neighbour_at(me, step, count)
        pl.semaphore_signal(barrier, inc=1, device_id={"inp": other}, device_id_type=MESH)
    pl.semaphore_signal(barrier, inc=1, device_id={"out": 1 - core}, device_id_type=MESH)

    token_f = tok_ref[...].astype(jnp.float32)
    gain = gain_ref[...].astype(jnp.float32)
    x_buf[...] = (token_f * gain).astype(jnp.bfloat16)
    squares[me] = jnp.broadcast_to(
        jnp.sum(token_f * token_f, axis=1, keepdims=True), (rows, HEAD_SIZE)
    )

    pl.semaphore_wait(barrier, count)
    for step in range(count - 1, 0, -1):
        sq_copy(neighbour_at(me, step, count)).start()

    half = HEAD_SIZE // 2
    row_at = lax.broadcasted_iota(jnp.int32, (rows, HEAD_SIZE), 0)
    lane_at = lax.broadcasted_iota(jnp.int32, (rows, HEAD_SIZE), 1)
    position = jnp.zeros((rows, HEAD_SIZE), jnp.int32)
    for row in range(rows):
        position = jnp.where(row_at == row, pos_ref[row], position)
    index_f = jnp.where(lane_at < half, lane_at, lane_at - half).astype(jnp.float32)
    freq = jnp.exp(index_f * jnp.float32(-2.0 * math.log(THETA) / HEAD_SIZE))
    angle = position.astype(jnp.float32) * freq
    cosine = jnp.cos(angle)
    sine = jnp.sin(angle)
    sine = jnp.where(lane_at < half, -sine, sine)

    def rotate(block):
        return (block * cosine + pltpu.roll(block, half, 1) * sine).astype(jnp.bfloat16)

    wk_copy().wait()
    wv_copy().wait()
    kv_part = jnp.dot(x_buf[...], wkv[...], preferred_element_type=jnp.float32)
    for head in range(kv_heads):
        kv_buf[head, :, 0:HEAD_SIZE] = kv_part[:, head * HEAD_SIZE : (head + 1) * HEAD_SIZE]
        kv_buf[head, :, HEAD_SIZE : 2 * HEAD_SIZE] = kv_part[
            :, kv_width + head * HEAD_SIZE : kv_width + (head + 1) * HEAD_SIZE
        ]

    def project(chunk):
        wq_copy(chunk).wait()
        wo_copy(chunk).start()
        q_part = jnp.dot(x_buf[...], wq[chunk], preferred_element_type=jnp.float32)
        whole = jnp.concatenate([q_part, kv_buf[chunk // per_kv]], axis=1)
        cut = whole.shape[1] // 2
        return jnp.concatenate([whole[:, :cut], whole[:, cut:]], axis=0)

    def project_step(at, carry):
        other = neighbour_at(me, count - 1 - at, count)
        part_out[other] = project(other).astype(jnp.bfloat16)
        part_copy(other).start()
        return carry

    lax.fori_loop(0, count - 1, project_step, 0)
    own_part[...] = project(me)

    for step in range(1, count):
        arrival(squares, sq_send, sq_recv, neighbour_at(me, step, count)).wait_recv()
    total_sq = squares[0]
    for at in range(1, count):
        total_sq = total_sq + squares[at]
    scale = lax.rsqrt(total_sq / MODEL_WIDTH + 1e-05)

    total = own_part[...]
    for step in range(1, count):
        other = neighbour_at(me, step, count)
        arrival(part_in, part_send, part_recv, other).wait_recv()
        total = total + part_in[other].astype(jnp.float32)
    blocks = []
    for side in range(2):
        for at in range(total.shape[1] // HEAD_SIZE):
            piece = total[side * rows : (side + 1) * rows, at * HEAD_SIZE : (at + 1) * HEAD_SIZE]
            blocks.append((piece * scale).astype(jnp.bfloat16).astype(jnp.float32))
    query = jnp.concatenate([rotate(blocks[head]) for head in range(heads)], axis=0)
    keys = rotate(blocks[heads])
    values = blocks[heads + 1].astype(jnp.bfloat16)
    scores = lax.dot_general(
        query, keys, (((1,), (1,)), ((), ())), preferred_element_type=jnp.float32
    ) / math.sqrt(HEAD_SIZE)
    cols = lane_at[:, :rows]
    distance = row_at[:, :rows] - cols
    allowed = jnp.where((distance >= 0) & (distance <= position[:, :rows]), 1.0, 0.0)
    allowed = jnp.concatenate([allowed] * heads, axis=0)
    expo = jnp.exp(jnp.where(allowed > 0.5, scores, -1e30))
    probs = (expo / jnp.sum(expo, axis=1, keepdims=True)).astype(jnp.bfloat16)
    context = jnp.dot(probs, values, preferred_element_type=jnp.float32)
    half_heads = heads // 2
    sides = [
        jnp.concatenate(
            [
                context[(side * half_heads + at) * rows : (side * half_heads + at + 1) * rows]
                for at in range(half_heads)
            ],
            axis=1,
        )
        for side in range(2)
    ]
    ctx_all[me] = jnp.concatenate(sides, axis=0).astype(jnp.bfloat16)
    for step in range(count - 1, 0, -1):
        ctx_copy(neighbour_at(me, step, count)).start()

    def contribution(chunk):
        wo_copy(chunk).wait()
        packed = ctx_all[chunk].astype(jnp.float32)
        left = jnp.concatenate([packed[:rows], packed[rows:]], axis=1).astype(jnp.bfloat16)
        return jnp.dot(left, wo[chunk], preferred_element_type=jnp.float32)

    def output_step(step, acc):
        other = neighbour_at(me, step, count)
        arrival(ctx_all, ctx_send, ctx_recv, other).wait_recv()
        return acc + contribution(other)

    acc = lax.fori_loop(1, count, output_step, contribution(me))

    def pack(array, keep):
        cut = array.shape[1] // 2
        low, high = array[:, :cut], array[:, cut:]
        upper = lax.broadcasted_iota(jnp.int32, low.shape, 0) < rows // 2
        first = jnp.where(upper, low, pltpu.roll(high, rows // 2, 0))
        second = jnp.where(upper, pltpu.roll(low, rows // 2, 0), high)
        return jnp.where(keep == 0, first, second)

    swap_out[...] = pack(acc, 1 - core)
    swap = pltpu.make_async_remote_copy(
        src_ref=swap_out,
        dst_ref=swap_in,
        send_sem=swap_sem.at[0],
        recv_sem=swap_sem.at[1],
        device_id={"out": 1 - core},
        device_id_type=MESH,
    )
    swap.start()
    mine = pack(acc, core)
    residual = pack(tok_ref[...].astype(jnp.float32), core)
    swap.wait_recv()
    result = (mine + swap_in[...] + residual).astype(jnp.bfloat16)
    cut = result.shape[1]
    out_ref[:, :cut] = result[: rows // 2]
    out_ref[:, cut:] = result[rows // 2 :]

    swap.wait_send()
    for step in range(1, count):
        other = neighbour_at(me, step, count)
        sq_copy(other).wait_send()
        part_copy(other).wait_send()
        ctx_copy(other).wait_send()


def fused(count, tokens, norm_gain, positions, w_query, key_weight, value_weight, w_output):
    rows, depth = tokens.shape
    query_width = w_query.shape[1]
    width = query_width // count
    kv_width = key_weight.shape[1]
    out_width = w_output.shape[1]
    packed = (width + 2 * HEAD_SIZE) // 2
    hbm = pl.BlockSpec(memory_space=pl.ANY)
    vmem = pl.BlockSpec(memory_space=pltpu.VMEM)
    dma = pltpu.SemaphoreType.DMA
    return pl.pallas_call(
        functools.partial(fused_kernel, count),
        out_shape=jax.ShapeDtypeStruct((rows // 2, out_width), jnp.bfloat16),
        in_specs=[pl.BlockSpec(memory_space=pltpu.SMEM), vmem, vmem, hbm, hbm, hbm, hbm],
        out_specs=vmem,
        scratch_shapes=[
            pltpu.VMEM((count, depth, width), jnp.bfloat16),
            pltpu.VMEM((depth, 2 * kv_width), jnp.bfloat16),
            pltpu.VMEM((count, width, out_width), jnp.bfloat16),
            pltpu.VMEM((rows, depth), jnp.bfloat16),
            pltpu.VMEM((kv_width // HEAD_SIZE, rows, 2 * HEAD_SIZE), jnp.float32),
            pltpu.VMEM((count, rows, HEAD_SIZE), jnp.float32),
            pltpu.VMEM((count, 2 * rows, packed), jnp.bfloat16),
            pltpu.VMEM((count, 2 * rows, packed), jnp.bfloat16),
            pltpu.VMEM((2 * rows, packed), jnp.float32),
            pltpu.VMEM((count, 2 * rows, width // 2), jnp.bfloat16),
            pltpu.VMEM((rows, out_width // 2), jnp.float32),
            pltpu.VMEM((rows, out_width // 2), jnp.float32),
            dma((count,)),
            dma((2,)),
            dma((count,)),
            dma((count,)),
            dma((count,)),
            dma((count,)),
            dma((count,)),
            dma((count,)),
            dma((count,)),
            dma((2,)),
        ],
        compiler_params=pltpu.CompilerParams(
            collective_id=0, has_side_effects=True, vmem_limit_bytes=56 * 1024 * 1024
        ),
    )(positions, tokens, norm_gain.reshape(1, depth), w_query, key_weight, value_weight, w_output)


def block(count, cores, tokens, norm_gain, positions, w_query, key_weight, value_weight, w_output):
    rows, depth = tokens.shape
    query_width = w_query.shape[1]
    kv_heads = key_weight.shape[1] // HEAD_SIZE
    held = 2 * (w_query.size + w_output.size + 2 * key_weight.size)
    fits = (
        rows == 8
        and cores == 2
        and query_width % (2 * HEAD_SIZE * count) == 0
        and count % kv_heads == 0
        and held <= 40 * 1024 * 1024
    )
    form = functools.partial(fused, count) if fits else shards
    return form(tokens, norm_gain, positions, w_query, key_weight, value_weight, w_output)


def solution(mesh):
    return jax.shard_map(
        functools.partial(block, mesh.shape["inp"], mesh.shape["out"]),
        mesh=mesh,
        in_specs=(
            P("groups", "inp"),
            P("inp"),
            P("groups"),
            P("inp", "out"),
            P("inp", "out"),
            P("inp", "out"),
            P("out", "inp"),
        ),
        out_specs=P(("groups", "out"), "inp"),
        check_vma=False,
    )
```

```python
import functools
import math

import jax
import jax.numpy as jnp
from jax import lax
from jax.experimental import pallas as pl
from jax.experimental.pallas import tpu as pltpu
from jax.sharding import PartitionSpec as P

MODEL_WIDTH = 16384
HEAD_SIZE = 128


THETA = 500000.0


def apply_rotary(flat, pos):
    rows = flat.shape[0]
    heads = flat.shape[1] // HEAD_SIZE
    half = HEAD_SIZE // 2
    shaped = flat.astype(jnp.float32).reshape(rows, heads, HEAD_SIZE)
    index_f = jnp.arange(half, dtype=jnp.float32)
    freq = jnp.exp(-jnp.log(jnp.float32(THETA)) * 2.0 * index_f / (2.0 * half))
    angle = pos.astype(jnp.float32)[:, None] * freq[None, :]
    cosine = jnp.cos(angle)[:, None, :]
    sine = jnp.sin(angle)[:, None, :]
    first = shaped[..., :half]
    second = shaped[..., half:]
    turned = jnp.concatenate(
        [first * cosine - second * sine, second * cosine + first * sine], axis=-1
    )
    return turned.reshape(rows, heads * HEAD_SIZE).astype(jnp.bfloat16)


def attend(rotated_query, row_pos, row_index, rotated_keys, value_matrix):
    rows = rotated_query.shape[0]
    partial_total = rotated_keys.shape[0]
    kv_heads = rotated_keys.shape[1] // HEAD_SIZE
    query_group = rotated_query.shape[1] // HEAD_SIZE // kv_heads
    q_shaped = rotated_query.reshape(rows, kv_heads, query_group, HEAD_SIZE)
    k_shaped = rotated_keys.reshape(partial_total, kv_heads, HEAD_SIZE)
    v_shaped = value_matrix.reshape(partial_total, kv_heads, HEAD_SIZE)
    scores = jnp.einsum("rkgd,skd->rkgs", q_shaped, k_shaped, preferred_element_type=jnp.float32)
    scores = scores / jnp.sqrt(jnp.float32(HEAD_SIZE))
    cols = jnp.arange(partial_total, dtype=jnp.int32)[None, :]
    allowed = (cols <= row_index[:, None]) & (row_index[:, None] - cols <= row_pos[:, None])
    scores = jnp.where(allowed[:, None, None, :], scores, jnp.float32(-1e30))
    expo = jnp.exp(scores)
    probs = (expo / jnp.sum(expo, axis=-1, keepdims=True)).astype(jnp.bfloat16)
    context = jnp.einsum("rkgs,skd->rkgd", probs, v_shaped, preferred_element_type=jnp.float32)
    return context.astype(jnp.bfloat16).reshape(rows, kv_heads * query_group * HEAD_SIZE)


def shards(tokens, norm_gain, positions, w_query, key_weight, value_weight, w_output):
    partial_total = tokens.shape[0]
    token_f = tokens.astype(jnp.float32)
    squares = lax.psum(jnp.sum(token_f * token_f, axis=1), "inp")
    scale = lax.rsqrt(squares / MODEL_WIDTH + 1e-05)
    normed = (token_f * scale[:, None] * norm_gain.astype(jnp.float32)[None, :]).astype(
        jnp.bfloat16
    )
    query_width = w_query.shape[1]
    q_part = jnp.dot(normed, w_query, preferred_element_type=jnp.float32)
    k_part = jnp.dot(normed, key_weight, preferred_element_type=jnp.float32)
    v_part = jnp.dot(normed, value_weight, preferred_element_type=jnp.float32)
    q_sum, k_sum, v_sum = lax.psum((q_part, k_part, v_part), "inp")
    rotated_query = apply_rotary(q_sum.astype(jnp.bfloat16), positions)
    rotated_keys = apply_rotary(k_sum.astype(jnp.bfloat16), positions)
    value_matrix = v_sum.astype(jnp.bfloat16)
    block_rows = min(partial_total, 128)
    blocks = partial_total // block_rows
    index_all = jnp.arange(partial_total, dtype=jnp.int32)

    def one_block(packed):
        q_block, pos_block, index_block = packed
        return attend(q_block, pos_block, index_block, rotated_keys, value_matrix)

    context = lax.map(
        one_block,
        (
            rotated_query.reshape(blocks, block_rows, query_width),
            positions.reshape(blocks, block_rows),
            index_all.reshape(blocks, block_rows),
        ),
    )
    context = context.reshape(partial_total, query_width)
    partial_out = jnp.dot(context, w_output, preferred_element_type=jnp.float32)
    reduced = lax.psum_scatter(partial_out, "out", scatter_dimension=0, tiled=True)
    half_rows = reduced.shape[0]
    residual = lax.dynamic_slice_in_dim(token_f, lax.axis_index("out") * half_rows, half_rows, 0)
    return (reduced + residual).astype(jnp.bfloat16)


MESH = pl.DeviceIdType.MESH


def neighbour_at(me, step, count):
    offset = ((step + 1) // 2) * (2 * (step % 2) - 1)
    return (me + offset + count) % count


def fused_kernel(
    count,
    pos_hbm,
    tok_hbm,
    gain_hbm,
    wq_hbm,
    wk_hbm,
    wv_hbm,
    wo_hbm,
    out_ref,
    pos_ref,
    tok_ref,
    gain_ref,
    wq,
    wkv,
    wo,
    x_buf,
    kv_buf,
    part_out,
    part_in,
    own_part,
    ctx_all,
    swap_out,
    swap_in,
    wq_sem,
    wkv_sem,
    wo_sem,
    small_sem,
    part_send,
    part_recv,
    ctx_send,
    ctx_recv,
    swap_sem,
):
    me = lax.axis_index("inp")
    core = lax.axis_index("out")
    partners = [neighbour_at(me, step, count) for step in range(count)]
    rows = tok_ref.shape[0]
    width = wq.shape[2]
    heads = width // HEAD_SIZE
    kv_width = wk_hbm.shape[1]
    kv_heads = kv_width // HEAD_SIZE
    per_kv = count // kv_heads

    def wq_copy(chunk):
        cols = pl.ds(pl.multiple_of(chunk * width, width), width)
        return pltpu.make_async_copy(wq_hbm.at[:, cols], wq.at[chunk], wq_sem.at[chunk])

    def wo_copy(chunk):
        at = pl.ds(pl.multiple_of(chunk * width, width), width)
        return pltpu.make_async_copy(wo_hbm.at[at, :], wo.at[chunk], wo_sem.at[chunk])

    def wk_copy():
        return pltpu.make_async_copy(wk_hbm, wkv.at[:, 0:kv_width], wkv_sem.at[0])

    def wv_copy():
        return pltpu.make_async_copy(wv_hbm, wkv.at[:, kv_width : 2 * kv_width], wkv_sem.at[1])

    def part_copy(other):
        return pltpu.make_async_remote_copy(
            src_ref=part_out.at[other],
            dst_ref=part_in.at[me],
            send_sem=part_send.at[other],
            recv_sem=part_recv.at[me],
            device_id={"inp": other},
            device_id_type=MESH,
        )

    def ctx_copy(other):
        return pltpu.make_async_remote_copy(
            src_ref=ctx_all.at[me],
            dst_ref=ctx_all.at[me],
            send_sem=ctx_send.at[other],
            recv_sem=ctx_recv.at[me],
            device_id={"inp": other},
            device_id_type=MESH,
        )

    def arrival(buffer, send, recv, other):
        return pltpu.make_async_remote_copy(
            src_ref=buffer.at[other],
            dst_ref=buffer.at[other],
            send_sem=send.at[other],
            recv_sem=recv.at[other],
            device_id={"inp": other},
            device_id_type=MESH,
        )

    barrier = pltpu.get_barrier_semaphore()
    for step in range(1, count):
        other = partners[step]
        pl.semaphore_signal(barrier, inc=1, device_id={"inp": other}, device_id_type=MESH)
    pl.semaphore_signal(barrier, inc=1, device_id={"out": 1 - core}, device_id_type=MESH)

    small = [
        pltpu.make_async_copy(tok_hbm, tok_ref, small_sem.at[0]),
        pltpu.make_async_copy(gain_hbm, gain_ref, small_sem.at[1]),
        pltpu.make_async_copy(pos_hbm, pos_ref, small_sem.at[2]),
    ]
    for copy in small:
        copy.start()
    wk_copy().start()
    wv_copy().start()
    for step in range(count - 1, -1, -1):
        wq_copy(partners[step]).start()

    for copy in small:
        copy.wait()
    token_f = tok_ref[...].astype(jnp.float32)
    gain = gain_ref[...].astype(jnp.float32).reshape(1, -1)
    x_buf[...] = (token_f * gain).astype(jnp.bfloat16)
    squares = jnp.broadcast_to(
        jnp.sum(token_f * token_f, axis=1, keepdims=True), (rows, HEAD_SIZE)
    )
    high = squares.astype(jnp.bfloat16).astype(jnp.float32)
    squares = jnp.concatenate([high, squares - high], axis=0)

    half = HEAD_SIZE // 2
    row_at = lax.broadcasted_iota(jnp.int32, (rows, HEAD_SIZE), 0)
    lane_at = lax.broadcasted_iota(jnp.int32, (rows, HEAD_SIZE), 1)
    position = jnp.zeros((rows, HEAD_SIZE), jnp.int32)
    for row in range(rows):
        position = jnp.where(row_at == row, pos_ref[row], position)
    index_f = jnp.where(lane_at < half, lane_at, lane_at - half).astype(jnp.float32)
    freq = jnp.exp(index_f * jnp.float32(-2.0 * math.log(THETA) / HEAD_SIZE))
    angle = position.astype(jnp.float32) * freq
    cosine = jnp.cos(angle)
    sine = jnp.sin(angle)
    sine = jnp.where(lane_at < half, -sine, sine)

    def rotate(block):
        return (block * cosine + pltpu.roll(block, half, 1) * sine).astype(jnp.bfloat16)

    wk_copy().wait()
    wv_copy().wait()
    kv_part = jnp.dot(x_buf[...], wkv[...], preferred_element_type=jnp.float32)
    for head in range(kv_heads):
        kv_buf[head, :, 0:HEAD_SIZE] = kv_part[:, head * HEAD_SIZE : (head + 1) * HEAD_SIZE]
        kv_buf[head, :, HEAD_SIZE : 2 * HEAD_SIZE] = kv_part[
            :, kv_width + head * HEAD_SIZE : kv_width + (head + 1) * HEAD_SIZE
        ]

    def project(chunk):
        wq_copy(chunk).wait()
        wo_copy(chunk).start()
        q_part = jnp.dot(x_buf[...], wq[chunk], preferred_element_type=jnp.float32)
        whole = jnp.concatenate([q_part, kv_buf[chunk // per_kv]], axis=1)
        cut = whole.shape[1] // 2
        folded = jnp.concatenate([whole[:, :cut], whole[:, cut:]], axis=0)
        return jnp.concatenate([folded, squares], axis=1)

    early = min(2, count - 2)
    for at in range(count - 1):
        other = partners[count - 1 - at]
        part_out[other] = project(other).astype(jnp.bfloat16)
        if at == early:
            pl.semaphore_wait(barrier, count)
            for before in range(early):
                part_copy(partners[count - 1 - before]).start()
        if at >= early:
            part_copy(other).start()
    own_part[...] = project(me)

    total = own_part[...]
    for step in range(1, count):
        other = partners[step]
        arrival(part_in, part_send, part_recv, other).wait_recv()
        total = total + part_in[other].astype(jnp.float32)
    columns = total.shape[1] // HEAD_SIZE - 1
    total_sq = total[:, columns * HEAD_SIZE :]
    total_sq = total_sq[:rows] + total_sq[rows:]
    scale = lax.rsqrt(total_sq / MODEL_WIDTH + 1e-05)
    blocks = []
    for side in range(2):
        for at in range(columns):
            piece = total[side * rows : (side + 1) * rows, at * HEAD_SIZE : (at + 1) * HEAD_SIZE]
            blocks.append((piece * scale).astype(jnp.bfloat16).astype(jnp.float32))
    query = jnp.concatenate([rotate(blocks[head]) for head in range(heads)], axis=0)
    keys = rotate(blocks[heads])
    values = blocks[heads + 1].astype(jnp.bfloat16)
    scores = lax.dot_general(
        query, keys, (((1,), (1,)), ((), ())), preferred_element_type=jnp.float32
    ) / math.sqrt(HEAD_SIZE)
    cols = lane_at[:, :rows]
    distance = row_at[:, :rows] - cols
    allowed = jnp.where((distance >= 0) & (distance <= position[:, :rows]), 1.0, 0.0)
    allowed = jnp.concatenate([allowed] * heads, axis=0)
    expo = jnp.exp(jnp.where(allowed > 0.5, scores, -1e30))
    probs = (expo / jnp.sum(expo, axis=1, keepdims=True)).astype(jnp.bfloat16)
    context = jnp.dot(probs, values, preferred_element_type=jnp.float32)
    half_heads = heads // 2
    sides = [
        jnp.concatenate(
            [
                context[(side * half_heads + at) * rows : (side * half_heads + at + 1) * rows]
                for at in range(half_heads)
            ],
            axis=1,
        )
        for side in range(2)
    ]
    ctx_all[me] = jnp.concatenate(sides, axis=0).astype(jnp.bfloat16)
    for step in range(count - 1, 0, -1):
        ctx_copy(partners[step]).start()

    def contribution(chunk):
        wo_copy(chunk).wait()
        packed = ctx_all[chunk].astype(jnp.float32)
        left = jnp.concatenate([packed[:rows], packed[rows:]], axis=1).astype(jnp.bfloat16)
        return jnp.dot(left, wo[chunk], preferred_element_type=jnp.float32)

    acc = contribution(me)
    for step in range(1, count):
        other = partners[step]
        arrival(ctx_all, ctx_send, ctx_recv, other).wait_recv()
        acc = acc + contribution(other)

    def pack(array, keep):
        cut = array.shape[1] // 2
        low, high = array[:, :cut], array[:, cut:]
        upper = lax.broadcasted_iota(jnp.int32, low.shape, 0) < rows // 2
        first = jnp.where(upper, low, pltpu.roll(high, rows // 2, 0))
        second = jnp.where(upper, pltpu.roll(low, rows // 2, 0), high)
        return jnp.where(keep == 0, first, second)

    swap_out[...] = pack(acc, 1 - core)
    swap = pltpu.make_async_remote_copy(
        src_ref=swap_out,
        dst_ref=swap_in,
        send_sem=swap_sem.at[0],
        recv_sem=swap_sem.at[1],
        device_id={"out": 1 - core},
        device_id_type=MESH,
    )
    swap.start()
    mine = pack(acc, core)
    residual = pack(tok_ref[...].astype(jnp.float32), core)
    swap.wait_recv()
    result = (mine + swap_in[...] + residual).astype(jnp.bfloat16)
    cut = result.shape[1]
    out_ref[:, :cut] = result[: rows // 2]
    out_ref[:, cut:] = result[rows // 2 :]

    swap.wait_send()
    for step in range(1, count):
        other = partners[step]
        part_copy(other).wait_send()
        ctx_copy(other).wait_send()


def fused(count, tokens, norm_gain, positions, w_query, key_weight, value_weight, w_output):
    rows, depth = tokens.shape
    query_width = w_query.shape[1]
    width = query_width // count
    kv_width = key_weight.shape[1]
    out_width = w_output.shape[1]
    packed = (width + 2 * HEAD_SIZE) // 2 + HEAD_SIZE
    hbm = pl.BlockSpec(memory_space=pl.ANY)
    vmem = pl.BlockSpec(memory_space=pltpu.VMEM)
    dma = pltpu.SemaphoreType.DMA
    return pl.pallas_call(
        functools.partial(fused_kernel, count),
        out_shape=jax.ShapeDtypeStruct((rows // 2, out_width), jnp.bfloat16),
        in_specs=[hbm] * 7,
        out_specs=vmem,
        scratch_shapes=[
            pltpu.SMEM((rows,), jnp.int32),
            pltpu.VMEM((rows, depth), jnp.bfloat16),
            pltpu.VMEM((depth,), jnp.bfloat16),
            pltpu.VMEM((count, depth, width), jnp.bfloat16),
            pltpu.VMEM((depth, 2 * kv_width), jnp.bfloat16),
            pltpu.VMEM((count, width, out_width), jnp.bfloat16),
            pltpu.VMEM((rows, depth), jnp.bfloat16),
            pltpu.VMEM((kv_width // HEAD_SIZE, rows, 2 * HEAD_SIZE), jnp.float32),
            pltpu.VMEM((count, 2 * rows, packed), jnp.bfloat16),
            pltpu.VMEM((count, 2 * rows, packed), jnp.bfloat16),
            pltpu.VMEM((2 * rows, packed), jnp.float32),
            pltpu.VMEM((count, 2 * rows, width // 2), jnp.bfloat16),
            pltpu.VMEM((rows, out_width // 2), jnp.float32),
            pltpu.VMEM((rows, out_width // 2), jnp.float32),
            dma((count,)),
            dma((2,)),
            dma((count,)),
            dma((3,)),
            dma((count,)),
            dma((count,)),
            dma((count,)),
            dma((count,)),
            dma((2,)),
        ],
        compiler_params=pltpu.CompilerParams(
            collective_id=0, has_side_effects=True, vmem_limit_bytes=56 * 1024 * 1024
        ),
    )(positions, tokens, norm_gain, w_query, key_weight, value_weight, w_output)


def block(count, cores, tokens, norm_gain, positions, w_query, key_weight, value_weight, w_output):
    rows, depth = tokens.shape
    query_width = w_query.shape[1]
    kv_heads = key_weight.shape[1] // HEAD_SIZE
    held = 2 * (w_query.size + w_output.size + 2 * key_weight.size)
    fits = (
        rows == 8
        and cores == 2
        and query_width % (2 * HEAD_SIZE * count) == 0
        and count % kv_heads == 0
        and held <= 40 * 1024 * 1024
    )
    form = functools.partial(fused, count) if fits else shards
    return form(tokens, norm_gain, positions, w_query, key_weight, value_weight, w_output)


def solution(mesh):
    return jax.shard_map(
        functools.partial(block, mesh.shape["inp"], mesh.shape["out"]),
        mesh=mesh,
        in_specs=(
            P("groups", "inp"),
            P("inp"),
            P("groups"),
            P("inp", "out"),
            P("inp", "out"),
            P("inp", "out"),
            P("out", "inp"),
        ),
        out_specs=P(("groups", "out"), "inp"),
        check_vma=False,
    )
```

```python
import functools
import math

import jax
import jax.numpy as jnp
from jax import lax
from jax.experimental import pallas as pl
from jax.experimental.pallas import tpu as pltpu
from jax.sharding import PartitionSpec as P

MODEL_WIDTH = 16384
HEAD_SIZE = 128


THETA = 500000.0


def apply_rotary(flat, pos):
    rows = flat.shape[0]
    heads = flat.shape[1] // HEAD_SIZE
    half = HEAD_SIZE // 2
    shaped = flat.astype(jnp.float32).reshape(rows, heads, HEAD_SIZE)
    index_f = jnp.arange(half, dtype=jnp.float32)
    freq = jnp.exp(-jnp.log(jnp.float32(THETA)) * 2.0 * index_f / (2.0 * half))
    angle = pos.astype(jnp.float32)[:, None] * freq[None, :]
    cosine = jnp.cos(angle)[:, None, :]
    sine = jnp.sin(angle)[:, None, :]
    first = shaped[..., :half]
    second = shaped[..., half:]
    turned = jnp.concatenate(
        [first * cosine - second * sine, second * cosine + first * sine], axis=-1
    )
    return turned.reshape(rows, heads * HEAD_SIZE).astype(jnp.bfloat16)


def attend(rotated_query, row_pos, row_index, rotated_keys, value_matrix):
    rows = rotated_query.shape[0]
    partial_total = rotated_keys.shape[0]
    kv_heads = rotated_keys.shape[1] // HEAD_SIZE
    query_group = rotated_query.shape[1] // HEAD_SIZE // kv_heads
    q_shaped = rotated_query.reshape(rows, kv_heads, query_group, HEAD_SIZE)
    k_shaped = rotated_keys.reshape(partial_total, kv_heads, HEAD_SIZE)
    v_shaped = value_matrix.reshape(partial_total, kv_heads, HEAD_SIZE)
    scores = jnp.einsum("rkgd,skd->rkgs", q_shaped, k_shaped, preferred_element_type=jnp.float32)
    scores = scores / jnp.sqrt(jnp.float32(HEAD_SIZE))
    cols = jnp.arange(partial_total, dtype=jnp.int32)[None, :]
    allowed = (cols <= row_index[:, None]) & (row_index[:, None] - cols <= row_pos[:, None])
    scores = jnp.where(allowed[:, None, None, :], scores, jnp.float32(-1e30))
    expo = jnp.exp(scores)
    probs = (expo / jnp.sum(expo, axis=-1, keepdims=True)).astype(jnp.bfloat16)
    context = jnp.einsum("rkgs,skd->rkgd", probs, v_shaped, preferred_element_type=jnp.float32)
    return context.astype(jnp.bfloat16).reshape(rows, kv_heads * query_group * HEAD_SIZE)


def shards(tokens, norm_gain, positions, w_query, key_weight, value_weight, w_output):
    partial_total = tokens.shape[0]
    token_f = tokens.astype(jnp.float32)
    squares = lax.psum(jnp.sum(token_f * token_f, axis=1), "inp")
    scale = lax.rsqrt(squares / MODEL_WIDTH + 1e-05)
    normed = (token_f * scale[:, None] * norm_gain.astype(jnp.float32)[None, :]).astype(
        jnp.bfloat16
    )
    query_width = w_query.shape[1]
    q_part = jnp.dot(normed, w_query, preferred_element_type=jnp.float32)
    k_part = jnp.dot(normed, key_weight, preferred_element_type=jnp.float32)
    v_part = jnp.dot(normed, value_weight, preferred_element_type=jnp.float32)
    q_sum, k_sum, v_sum = lax.psum((q_part, k_part, v_part), "inp")
    rotated_query = apply_rotary(q_sum.astype(jnp.bfloat16), positions)
    rotated_keys = apply_rotary(k_sum.astype(jnp.bfloat16), positions)
    value_matrix = v_sum.astype(jnp.bfloat16)
    block_rows = min(partial_total, 128)
    blocks = partial_total // block_rows
    index_all = jnp.arange(partial_total, dtype=jnp.int32)

    def one_block(packed):
        q_block, pos_block, index_block = packed
        return attend(q_block, pos_block, index_block, rotated_keys, value_matrix)

    context = lax.map(
        one_block,
        (
            rotated_query.reshape(blocks, block_rows, query_width),
            positions.reshape(blocks, block_rows),
            index_all.reshape(blocks, block_rows),
        ),
    )
    context = context.reshape(partial_total, query_width)
    partial_out = jnp.dot(context, w_output, preferred_element_type=jnp.float32)
    reduced = lax.psum_scatter(partial_out, "out", scatter_dimension=0, tiled=True)
    half_rows = reduced.shape[0]
    residual = lax.dynamic_slice_in_dim(token_f, lax.axis_index("out") * half_rows, half_rows, 0)
    return (reduced + residual).astype(jnp.bfloat16)


MESH = pl.DeviceIdType.MESH


def neighbour_at(me, step, count):
    offset = ((step + 1) // 2) * (2 * (step % 2) - 1)
    return (me + offset + count) % count


def fused_kernel(
    count,
    pos_hbm,
    tok_hbm,
    gain_hbm,
    wq_hbm,
    wk_hbm,
    wv_hbm,
    wo_hbm,
    out_ref,
    pos_ref,
    tok_ref,
    gain_ref,
    wq,
    wkv,
    wo,
    x_buf,
    kv_buf,
    part_out,
    part_in,
    own_part,
    ctx_all,
    swap_out,
    swap_in,
    wq_sem,
    wkv_sem,
    wo_sem,
    small_sem,
    part_send,
    part_recv,
    ctx_send,
    ctx_recv,
    swap_sem,
):
    me = lax.axis_index("inp")
    core = lax.axis_index("out")
    partners = [neighbour_at(me, step, count) for step in range(count)]
    rows = tok_ref.shape[0]
    width = wq.shape[2]
    heads = width // HEAD_SIZE
    kv_width = wk_hbm.shape[1]
    kv_heads = kv_width // HEAD_SIZE
    per_kv = count // kv_heads

    def wq_copy(chunk):
        cols = pl.ds(pl.multiple_of(chunk * width, width), width)
        return pltpu.make_async_copy(wq_hbm.at[:, cols], wq.at[chunk], wq_sem.at[chunk])

    def wo_copy(chunk):
        at = pl.ds(pl.multiple_of(chunk * width, width), width)
        return pltpu.make_async_copy(wo_hbm.at[at, :], wo.at[chunk], wo_sem.at[chunk])

    def wk_copy():
        return pltpu.make_async_copy(wk_hbm, wkv.at[:, 0:kv_width], wkv_sem.at[0])

    def wv_copy():
        return pltpu.make_async_copy(wv_hbm, wkv.at[:, kv_width : 2 * kv_width], wkv_sem.at[1])

    def part_copy(other):
        return pltpu.make_async_remote_copy(
            src_ref=part_out.at[other],
            dst_ref=part_in.at[me],
            send_sem=part_send.at[other],
            recv_sem=part_recv.at[me],
            device_id={"inp": other},
            device_id_type=MESH,
        )

    def ctx_copy(other):
        return pltpu.make_async_remote_copy(
            src_ref=ctx_all.at[me],
            dst_ref=ctx_all.at[me],
            send_sem=ctx_send.at[other],
            recv_sem=ctx_recv.at[me],
            device_id={"inp": other},
            device_id_type=MESH,
        )

    def arrival(buffer, send, recv, other):
        return pltpu.make_async_remote_copy(
            src_ref=buffer.at[other],
            dst_ref=buffer.at[other],
            send_sem=send.at[other],
            recv_sem=recv.at[other],
            device_id={"inp": other},
            device_id_type=MESH,
        )

    barrier = pltpu.get_barrier_semaphore()
    for step in range(1, count):
        other = partners[step]
        pl.semaphore_signal(barrier, inc=1, device_id={"inp": other}, device_id_type=MESH)
    pl.semaphore_signal(barrier, inc=1, device_id={"out": 1 - core}, device_id_type=MESH)

    small = [
        pltpu.make_async_copy(tok_hbm, tok_ref, small_sem.at[0]),
        pltpu.make_async_copy(gain_hbm, gain_ref, small_sem.at[1]),
        pltpu.make_async_copy(pos_hbm, pos_ref, small_sem.at[2]),
    ]
    for copy in small:
        copy.start()
    wk_copy().start()
    wv_copy().start()
    for step in range(count - 1, -1, -1):
        wq_copy(partners[step]).start()

    for copy in small:
        copy.wait()
    token_f = tok_ref[...].astype(jnp.float32)
    gain = gain_ref[...].astype(jnp.float32).reshape(1, -1)
    x_buf[...] = (token_f * gain).astype(jnp.bfloat16)
    squares = jnp.broadcast_to(
        jnp.sum(token_f * token_f, axis=1, keepdims=True), (rows, HEAD_SIZE)
    )
    high = squares.astype(jnp.bfloat16).astype(jnp.float32)
    squares = jnp.concatenate([high, squares - high], axis=0)

    half = HEAD_SIZE // 2
    row_at = lax.broadcasted_iota(jnp.int32, (rows, HEAD_SIZE), 0)
    lane_at = lax.broadcasted_iota(jnp.int32, (rows, HEAD_SIZE), 1)
    position = jnp.zeros((rows, HEAD_SIZE), jnp.int32)
    for row in range(rows):
        position = jnp.where(row_at == row, pos_ref[row], position)
    index_f = jnp.where(lane_at < half, lane_at, lane_at - half).astype(jnp.float32)
    freq = jnp.exp(index_f * jnp.float32(-2.0 * math.log(THETA) / HEAD_SIZE))
    angle = position.astype(jnp.float32) * freq
    cosine = jnp.cos(angle)
    sine = jnp.sin(angle)
    sine = jnp.where(lane_at < half, -sine, sine)

    def rotate(block):
        return (block * cosine + pltpu.roll(block, half, 1) * sine).astype(jnp.bfloat16)

    wk_copy().wait()
    wv_copy().wait()
    kv_part = jnp.dot(x_buf[...], wkv[...], preferred_element_type=jnp.float32)
    for head in range(kv_heads):
        kv_buf[head, :, 0:HEAD_SIZE] = kv_part[:, head * HEAD_SIZE : (head + 1) * HEAD_SIZE]
        kv_buf[head, :, HEAD_SIZE : 2 * HEAD_SIZE] = kv_part[
            :, kv_width + head * HEAD_SIZE : kv_width + (head + 1) * HEAD_SIZE
        ]

    def project(chunk):
        wq_copy(chunk).wait()
        wo_copy(chunk).start()
        q_part = jnp.dot(x_buf[...], wq[chunk], preferred_element_type=jnp.float32)
        whole = jnp.concatenate([q_part, kv_buf[chunk // per_kv]], axis=1)
        cut = whole.shape[1] // 2
        folded = jnp.concatenate([whole[:, :cut], whole[:, cut:]], axis=0)
        return jnp.concatenate([folded, squares], axis=1)

    early = min(2, count - 2)
    for at in range(count - 1):
        other = partners[count - 1 - at]
        part_out[other] = project(other).astype(jnp.bfloat16)
        if at == early:
            pl.semaphore_wait(barrier, count)
            for before in range(early):
                part_copy(partners[count - 1 - before]).start()
        if at >= early:
            part_copy(other).start()
    own_part[...] = project(me)

    total = own_part[...]
    for step in range(1, count):
        other = partners[step]
        arrival(part_in, part_send, part_recv, other).wait_recv()
        total = total + part_in[other].astype(jnp.float32)
    columns = total.shape[1] // HEAD_SIZE - 1
    total_sq = total[:, columns * HEAD_SIZE :]
    total_sq = total_sq[:rows] + total_sq[rows:]
    scale = lax.rsqrt(total_sq / MODEL_WIDTH + 1e-05)
    blocks = []
    for side in range(2):
        for at in range(columns):
            piece = total[side * rows : (side + 1) * rows, at * HEAD_SIZE : (at + 1) * HEAD_SIZE]
            blocks.append((piece * scale).astype(jnp.bfloat16).astype(jnp.float32))
    query = jnp.concatenate([rotate(blocks[head]) for head in range(heads)], axis=0)
    keys = rotate(blocks[heads])
    values = blocks[heads + 1].astype(jnp.bfloat16)
    scores = lax.dot_general(
        query, keys, (((1,), (1,)), ((), ())), preferred_element_type=jnp.float32
    ) / math.sqrt(HEAD_SIZE)
    cols = lane_at[:, :rows]
    distance = row_at[:, :rows] - cols
    allowed = jnp.where((distance >= 0) & (distance <= position[:, :rows]), 1.0, 0.0)
    allowed = jnp.concatenate([allowed] * heads, axis=0)
    expo = jnp.exp(jnp.where(allowed > 0.5, scores, -1e30))
    probs = (expo / jnp.sum(expo, axis=1, keepdims=True)).astype(jnp.bfloat16)
    context = jnp.dot(probs, values, preferred_element_type=jnp.float32)
    half_heads = heads // 2
    sides = [
        jnp.concatenate(
            [
                context[(side * half_heads + at) * rows : (side * half_heads + at + 1) * rows]
                for at in range(half_heads)
            ],
            axis=1,
        )
        for side in range(2)
    ]
    ctx_all[me] = jnp.concatenate(sides, axis=0).astype(jnp.bfloat16)
    for step in range(count - 1, 0, -1):
        ctx_copy(partners[step]).start()

    def contribution(chunk):
        packed = ctx_all[chunk].astype(jnp.float32)
        left = jnp.concatenate([packed[:rows], packed[rows:]], axis=1).astype(jnp.bfloat16)
        return jnp.dot(left, wo[chunk], preferred_element_type=jnp.float32)

    wo_copy(me).wait()
    acc = contribution(me)
    for group in (partners[1 : count // 2], partners[count // 2 :]):
        for other in group:
            wo_copy(other).wait()
            arrival(ctx_all, ctx_send, ctx_recv, other).wait_recv()
        for other in group:
            acc = acc + contribution(other)

    def pack(array, keep):
        cut = array.shape[1] // 2
        low, high = array[:, :cut], array[:, cut:]
        upper = lax.broadcasted_iota(jnp.int32, low.shape, 0) < rows // 2
        first = jnp.where(upper, low, pltpu.roll(high, rows // 2, 0))
        second = jnp.where(upper, pltpu.roll(low, rows // 2, 0), high)
        return jnp.where(keep == 0, first, second)

    swap_out[...] = pack(acc, 1 - core)
    swap = pltpu.make_async_remote_copy(
        src_ref=swap_out,
        dst_ref=swap_in,
        send_sem=swap_sem.at[0],
        recv_sem=swap_sem.at[1],
        device_id={"out": 1 - core},
        device_id_type=MESH,
    )
    swap.start()
    mine = pack(acc, core)
    residual = pack(tok_ref[...].astype(jnp.float32), core)
    swap.wait_recv()
    result = (mine + swap_in[...] + residual).astype(jnp.bfloat16)
    cut = result.shape[1]
    out_ref[:, :cut] = result[: rows // 2]
    out_ref[:, cut:] = result[rows // 2 :]

    swap.wait_send()
    for step in range(1, count):
        other = partners[step]
        part_copy(other).wait_send()
        ctx_copy(other).wait_send()


def fused(count, tokens, norm_gain, positions, w_query, key_weight, value_weight, w_output):
    rows, depth = tokens.shape
    query_width = w_query.shape[1]
    width = query_width // count
    kv_width = key_weight.shape[1]
    out_width = w_output.shape[1]
    packed = (width + 2 * HEAD_SIZE) // 2 + HEAD_SIZE
    hbm = pl.BlockSpec(memory_space=pl.ANY)
    vmem = pl.BlockSpec(memory_space=pltpu.VMEM)
    dma = pltpu.SemaphoreType.DMA
    return pl.pallas_call(
        functools.partial(fused_kernel, count),
        out_shape=jax.ShapeDtypeStruct((rows // 2, out_width), jnp.bfloat16),
        in_specs=[hbm] * 7,
        out_specs=vmem,
        scratch_shapes=[
            pltpu.SMEM((rows,), jnp.int32),
            pltpu.VMEM((rows, depth), jnp.bfloat16),
            pltpu.VMEM((depth,), jnp.bfloat16),
            pltpu.VMEM((count, depth, width), jnp.bfloat16),
            pltpu.VMEM((depth, 2 * kv_width), jnp.bfloat16),
            pltpu.VMEM((count, width, out_width), jnp.bfloat16),
            pltpu.VMEM((rows, depth), jnp.bfloat16),
            pltpu.VMEM((kv_width // HEAD_SIZE, rows, 2 * HEAD_SIZE), jnp.float32),
            pltpu.VMEM((count, 2 * rows, packed), jnp.bfloat16),
            pltpu.VMEM((count, 2 * rows, packed), jnp.bfloat16),
            pltpu.VMEM((2 * rows, packed), jnp.float32),
            pltpu.VMEM((count, 2 * rows, width // 2), jnp.bfloat16),
            pltpu.VMEM((rows, out_width // 2), jnp.float32),
            pltpu.VMEM((rows, out_width // 2), jnp.float32),
            dma((count,)),
            dma((2,)),
            dma((count,)),
            dma((3,)),
            dma((count,)),
            dma((count,)),
            dma((count,)),
            dma((count,)),
            dma((2,)),
        ],
        compiler_params=pltpu.CompilerParams(
            collective_id=0, has_side_effects=True, vmem_limit_bytes=56 * 1024 * 1024
        ),
    )(positions, tokens, norm_gain, w_query, key_weight, value_weight, w_output)


def block(count, cores, tokens, norm_gain, positions, w_query, key_weight, value_weight, w_output):
    rows, depth = tokens.shape
    query_width = w_query.shape[1]
    kv_heads = key_weight.shape[1] // HEAD_SIZE
    held = 2 * (w_query.size + w_output.size + 2 * key_weight.size)
    fits = (
        rows == 8
        and cores == 2
        and query_width % (2 * HEAD_SIZE * count) == 0
        and count % kv_heads == 0
        and held <= 40 * 1024 * 1024
    )
    form = functools.partial(fused, count) if fits else shards
    return form(tokens, norm_gain, positions, w_query, key_weight, value_weight, w_output)


def solution(mesh):
    return jax.shard_map(
        functools.partial(block, mesh.shape["inp"], mesh.shape["out"]),
        mesh=mesh,
        in_specs=(
            P("groups", "inp"),
            P("inp"),
            P("groups"),
            P("inp", "out"),
            P("inp", "out"),
            P("inp", "out"),
            P("out", "inp"),
        ),
        out_specs=P(("groups", "out"), "inp"),
        check_vma=False,
    )
```
